256 devices in a mesh: group: 4 (over y_lo, core), dev: 64 (over x, z, y_hi).
Axes of the slice: x: 4, y: 4 (y_hi: 2, y_lo: 2; y = y_hi * 2 + y_lo), z: 8, core: 2. Of those that a mesh axis runs over, the one named last changes fastest.
Arguments:
- queries: bfloat16 [163840, 768], P(('group', 'dev')), may hold values from -24 to 24
- docids: bfloat16 [163840, 768], P(('group', 'dev')), may hold values from -6 to 6
- labels: int32 [163840], P(('group', 'dev')), may hold values from 0 to 163839, as said below
- head_query: bfloat16 [768, 768], replicated, may hold values from -0.21875 to 0.21875
- head_docid: bfloat16 [768, 768], replicated, may hold values from -0.21875 to 0.21875
Outputs:
- doc_update: bfloat16 [163840, 768], P(('group', 'dev'))
- query_head_step: float32 [768, 768], replicated
- docid_head_step: float32 [768, 768], replicated
The draws below stay inside these ranges and needn't reach their ends.
Inputs may be any that keep to these rules, and one draw needn't show every extreme that they name: `labels`: each query's positive docid lies in its own block or in one of its 4 source blocks.
All inputs are finite; a program needn't handle non-finite values.
Results may differ from the reference program's by a relative error of at most 0.0075.
Values may be sent and summed in bfloat16 or wider, within the bound.
No kernel may reach another device: no remote copies, remote signals or barrier semaphores. Data moves between devices by JAX's collectives and lax.ppermute only.
A program may use at most 128 MiB of HBM per device.

```python
import jax
import jax.numpy as jnp
import numpy as np
from jax import lax

D = 768
E = 768
TOK_DEV = 640
ROUNDS = 4
GROUPS = 4
DEVS = 64
TOKENS = 163840


def draw_labels(key, part):
    key = jax.random.fold_in(key, 17)
    round_key, offset_key = jax.random.split(key)
    all_rows = jnp.arange(TOKENS, dtype=jnp.int32)
    group_of = all_rows // (TOK_DEV * DEVS)
    device_of = all_rows // TOK_DEV % DEVS
    round_pick = jax.random.randint(round_key, (TOKENS,), 0, ROUNDS + 1).astype(jnp.int32)
    group_flip = jnp.where(round_pick == 0, 0, jnp.where((round_pick - 1) % 2 == 0, 1, 2)).astype(jnp.int32)
    source_group = jnp.bitwise_xor(group_of, group_flip)
    source_device = (device_of - round_pick) % DEVS
    offset = jax.random.randint(offset_key, (TOKENS,), 0, TOK_DEV).astype(jnp.int32)
    result = (source_group * DEVS + source_device) * TOK_DEV + offset
    result = result.at[0].set(0).at[TOKENS - 1].set(TOKENS - 1)
    return result.astype(jnp.int32)


def with_spikes(values, rng, source, target, parts, factor):
    owner, partner = [(jnp.arange(values.shape[dim]) // (values.shape[dim] // parts)).reshape([-1 if axis == dim else 1 for axis in range(values.ndim)]) for dim in (source, target)]
    chosen = jax.random.permutation(rng, parts)[partner]
    strong = (owner == chosen) | (owner == (partner + parts // 2) % parts)
    return jnp.where(strong, factor * values, values)


def level_of(rng, extent, cuts, smallest, high):
    gain, own = 1.0, jax.random.fold_in(rng, 6)
    for axis_at, shards_of in cuts:
        draws = jnp.exp(jax.random.uniform(jax.random.fold_in(own, axis_at), (shards_of,), jnp.float32, smallest / len(cuts), high / len(cuts)))
        gain = gain * jnp.repeat(draws, extent[axis_at] // shards_of).reshape([-1 if axis == axis_at else 1 for axis in range(len(extent))])
    return gain


def scatter_about(own_key, shape, scale, most, cuts=(), kind=jnp.bfloat16):
    drawn = jax.random.normal(own_key, shape, jnp.float32) * scale
    if len(cuts) > 0:
        drawn = level_of(own_key, shape, cuts, -0.22, 0.18) * drawn
    return jnp.clip(drawn, min=-most, max=most).astype(kind)


def gaussian_with(own_key, dims, spread, limit, pieces, heavy, held_as=jnp.bfloat16):
    values = spread * jax.random.normal(own_key, dims, jnp.float32)
    if pieces:
        values = values * level_of(own_key, dims, pieces, -0.22, 0.18)
    return jnp.clip(with_spikes(values, jax.random.fold_in(own_key, 3), *heavy), -limit, limit).astype(held_as)


def setup_inputs(seed: int = 0) -> dict:
    key_of = jax.random.split(jax.random.key(seed), 6)
    queries = gaussian_with(key_of[0], (TOKENS, D), 1.0, 24.0, ((0, 256),), (0, 1, 256, 6.0))
    docids = scatter_about(key_of[1], (TOKENS, D), 1.0, 6.0, ((0, 256),))
    labels = draw_labels(jax.random.fold_in(key_of[5], 71), 0)
    head_query = scatter_about(key_of[3], (D, E), D ** -0.5, 0.21875)
    head_docid = scatter_about(key_of[4], (D, E), D ** -0.5, 0.21875)
    return dict(queries=queries, docids=docids, labels=labels, head_query=head_query, head_docid=head_docid)


LOGIT_SCALE = 5.0
LOGIT_BIAS = -2.0
EPSILON = 1e-06

def project(inputs, weight):
    projected = jnp.dot(inputs, weight, preferred_element_type=jnp.float32)
    inverse = lax.rsqrt(lax.optimization_barrier(jnp.sum(projected * projected, axis=-1, keepdims=True)) + EPSILON)
    return (projected * inverse, inverse)

def pair_weights(query_block, docid_block, label_block, doc_starts):
    scores = jnp.einsum('nqe,nke->nqk', query_block.astype(jnp.float32), docid_block.astype(jnp.float32))
    logits = LOGIT_SCALE * scores + LOGIT_BIAS
    columns = doc_starts[:, None, None] + jnp.arange(TOK_DEV, dtype=jnp.int32)[None, None, :]
    target = jnp.where(label_block[:, :, None] == columns, 1.0, -1.0).astype(jnp.float32)
    rounded = (-target * jax.nn.sigmoid(-target * logits)).astype(jnp.bfloat16)
    return lax.optimization_barrier(rounded).astype(jnp.float32)

def direction(grad, unit, inverse):
    inner = lax.optimization_barrier(jnp.sum(unit * grad, axis=-1, keepdims=True))
    return ((grad - unit * inner) * inverse).astype(jnp.bfloat16)

def unit_rms(grad):
    return grad * lax.rsqrt(jnp.mean(grad * grad) + EPSILON)

def reference(queries, docids, labels, head_query, head_docid):
    query_unit, query_inverse = project(queries, head_query)
    docid_unit, docid_inverse = project(docids, head_docid)
    query_blocks = query_unit.astype(jnp.bfloat16).reshape(GROUPS, DEVS, TOK_DEV, E)
    docid_blocks = docid_unit.astype(jnp.bfloat16).reshape(GROUPS, DEVS, TOK_DEV, E)
    label_blocks = labels.reshape(GROUPS, DEVS, TOK_DEV)
    group_ids = np.arange(GROUPS)
    device_ids = np.arange(DEVS)
    query_terms = [jnp.zeros((DEVS, TOK_DEV, E), jnp.float32) for group_no in range(GROUPS)]
    docid_terms = [jnp.zeros((DEVS, TOK_DEV, E), jnp.float32) for group_no in range(GROUPS)]
    for round_no in range(ROUNDS + 1):
        if round_no == 0:
            source_groups = group_ids
        else:
            source_groups = group_ids ^ 1 << (round_no - 1) % 2
        sources = jnp.roll(docid_blocks[source_groups], round_no, axis=1)
        for group_no in range(GROUPS):
            source_group = int(source_groups[group_no])
            starts = jnp.asarray(((source_group * DEVS + (device_ids - round_no) % DEVS) * TOK_DEV).astype(np.int32)).astype(jnp.int32)
            weights = pair_weights(query_blocks[group_no], sources[group_no], label_blocks[group_no], starts)
            query_terms[group_no] = query_terms[group_no] + LOGIT_SCALE * jnp.einsum('nqk,nke->nqe', weights, sources[group_no].astype(jnp.float32))
            partial_terms = LOGIT_SCALE * jnp.einsum('nqk,nqe->nke', weights, query_blocks[group_no].astype(jnp.float32))
            if round_no == 0:
                docid_terms[group_no] = docid_terms[group_no] + partial_terms
            else:
                returned = jnp.roll(partial_terms.astype(jnp.bfloat16), -round_no, axis=0).astype(jnp.float32)
                docid_terms[source_group] = docid_terms[source_group] + returned
    query_grad = jnp.stack(query_terms).reshape(TOKENS, E)
    docid_grad = jnp.stack(docid_terms).reshape(TOKENS, E)
    query_direct = direction(query_grad, query_unit, query_inverse)
    docid_direct = direction(docid_grad, docid_unit, docid_inverse)
    query_head_grad = jnp.dot(queries.T, query_direct, preferred_element_type=jnp.float32)
    docid_head_grad = jnp.dot(docids.T, docid_direct, preferred_element_type=jnp.float32)
    doc_grad = jnp.dot(docid_direct, head_docid.T, preferred_element_type=jnp.float32)
    doc_update = (doc_grad * lax.rsqrt(lax.optimization_barrier(jnp.mean(doc_grad * doc_grad, axis=-1, keepdims=True)) + EPSILON)).astype(jnp.bfloat16)
    return (doc_update, unit_rms(query_head_grad), unit_rms(docid_head_grad))
```

```python
import jax
import jax.numpy as jnp
from jax import lax
from jax.sharding import Mesh
from jax.sharding import PartitionSpec as P

LOGIT_SCALE = 5.0
LOGIT_BIAS = -2.0
EPSILON = 1e-06

AXES = ("y_lo", "core", "x", "z", "y_hi")
SIZES = (2, 2, 4, 8, 2)
PLANE = ("y_lo", "y_hi", "x")
DEVS = 64


def moved(block, flip, shift):
    pairs = []
    for source in range(4 * DEVS):
        group, dev = divmod(source, DEVS)
        pairs.append((source, (group ^ flip) * DEVS + (dev + shift) % DEVS))
    return lax.ppermute(block, AXES, pairs)


def project(inputs, weight):
    projected = jnp.dot(inputs, weight, preferred_element_type=jnp.float32)
    inverse = lax.rsqrt(jnp.sum(projected * projected, axis=-1, keepdims=True) + EPSILON)
    return (projected * inverse, inverse)


def direction(grad, unit, inverse):
    inner = jnp.sum(unit * grad, axis=-1, keepdims=True)
    return ((grad - unit * inner) * inverse).astype(jnp.bfloat16)


def pair_weights(queries, docids, labels, doc_start):
    scores = lax.dot_general(
        queries, docids, (((1,), (1,)), ((), ())), preferred_element_type=jnp.float32
    )
    logits = LOGIT_SCALE * scores + LOGIT_BIAS
    columns = jnp.arange(docids.shape[0], dtype=jnp.int32)
    positive = labels[:, None] == doc_start + columns[None, :]
    return (jax.nn.sigmoid(logits) - jnp.where(positive, 1.0, 0.0)).astype(jnp.bfloat16)


def rows_of(weights, docids):
    return LOGIT_SCALE * jnp.dot(weights, docids, preferred_element_type=jnp.float32)


def columns_of(weights, queries):
    return LOGIT_SCALE * lax.dot_general(
        weights, queries, (((0,), (0,)), ((), ())), preferred_element_type=jnp.float32
    )


def total(partial):
    rows, width = partial.shape
    half = rows // 2
    core = lax.axis_index("core")
    first, second = partial[:half], partial[half:]
    kept = jnp.where(core == 0, first, second)
    sent = jnp.where(core == 0, second, first).astype(jnp.bfloat16)
    value = kept + moved(sent, 1, 0).astype(jnp.float32)
    plane, line = 16, SIZES[3]
    piece = value.astype(jnp.bfloat16).reshape(plane, half // plane, width)
    piece = lax.all_to_all(piece, PLANE, 0, 0, tiled=True)
    value = jnp.sum(piece.astype(jnp.float32), axis=0)
    piece = value.astype(jnp.bfloat16).reshape(line, -1, 128)
    piece = lax.all_to_all(piece, "z", 0, 0, tiled=True)
    value = jnp.sum(piece.astype(jnp.float32), axis=0).astype(jnp.bfloat16)
    piece = jnp.broadcast_to(value[None], (line,) + value.shape)
    piece = lax.all_to_all(piece, "z", 0, 0, tiled=True).reshape(half // plane, width)
    piece = jnp.broadcast_to(piece[None], (plane,) + piece.shape)
    mine = lax.all_to_all(piece, PLANE, 0, 0, tiled=True).reshape(half, width)
    other = moved(mine, 1, 0)
    first = jnp.where(core == 0, mine, other)
    second = jnp.where(core == 0, other, mine)
    return first.astype(jnp.float32), second.astype(jnp.float32)


def unit_rms(grad):
    return grad * lax.rsqrt(jnp.mean(grad * grad) + EPSILON)


def per_device(queries, docids, labels, head_query, head_docid):
    block_rows = queries.shape[0]
    group = lax.axis_index("y_lo") * 2 + lax.axis_index("core")
    dev = (lax.axis_index("x") * 8 + lax.axis_index("z")) * 2 + lax.axis_index("y_hi")

    def start(flip, shift):
        return (jnp.bitwise_xor(group, flip) * DEVS + (dev + shift) % DEVS) * block_rows

    docid_unit, docid_inverse = project(docids, head_docid)
    docid_vec = docid_unit.astype(jnp.bfloat16)
    docid_1 = moved(docid_vec, 1, 1)
    docid_2 = moved(docid_vec, 2, 2)
    query_unit, query_inverse = project(queries, head_query)
    query_vec = query_unit.astype(jnp.bfloat16)
    query_far = moved(query_vec, 0, -2)
    labels_far = moved(labels, 0, -2)

    weights = pair_weights(query_vec, docid_vec, labels, start(0, 0))
    query_grad = rows_of(weights, docid_vec)
    docid_grad = columns_of(weights, query_vec)

    both = jnp.concatenate([query_vec, query_far])
    labels_both = jnp.concatenate([labels, labels_far])
    weights_1 = pair_weights(both, docid_1, labels_both, start(1, -1))
    back_1 = moved(columns_of(weights_1, both).astype(jnp.bfloat16), 1, -1)
    query_both = rows_of(weights_1, docid_1)
    weights_2 = pair_weights(both, docid_2, labels_both, start(2, -2))
    back_2 = moved(columns_of(weights_2, both).astype(jnp.bfloat16), 2, -2)
    query_both = query_both + rows_of(weights_2, docid_2)
    back_far = moved(query_both[block_rows:].astype(jnp.bfloat16), 0, 2)
    query_grad = query_grad + query_both[:block_rows] + back_far.astype(jnp.float32)
    docid_grad = docid_grad + back_1.astype(jnp.float32) + back_2.astype(jnp.float32)

    query_direct = direction(query_grad, query_unit, query_inverse)
    docid_direct = direction(docid_grad, docid_unit, docid_inverse)
    query_head_grad = lax.dot_general(
        queries, query_direct, (((0,), (0,)), ((), ())), preferred_element_type=jnp.float32
    )
    docid_head_grad = lax.dot_general(
        docids, docid_direct, (((0,), (0,)), ((), ())), preferred_element_type=jnp.float32
    )
    query_total, docid_total = total(jnp.concatenate([query_head_grad, docid_head_grad]))
    query_head_step = unit_rms(query_total)
    docid_head_step = unit_rms(docid_total)
    doc_grad = lax.dot_general(
        docid_direct, head_docid, (((1,), (1,)), ((), ())), preferred_element_type=jnp.float32
    )
    doc_update = (
        doc_grad * lax.rsqrt(jnp.mean(doc_grad * doc_grad, axis=-1, keepdims=True) + EPSILON)
    ).astype(jnp.bfloat16)
    return (doc_update, query_head_step, docid_head_step)


def solution(mesh):
    split = Mesh(mesh.devices.reshape(SIZES), AXES)
    rows = P(AXES)
    return jax.shard_map(
        per_device,
        mesh=split,
        in_specs=(rows, rows, rows, P(), P()),
        out_specs=(rows, P(), P()),
        check_vma=False,
    )
```

```python
import functools

import jax
import jax.numpy as jnp
from jax import lax
from jax.experimental import pallas as pl
from jax.experimental.pallas import tpu as pltpu
from jax.sharding import Mesh
from jax.sharding import PartitionSpec as P

LOGIT_SCALE = 5.0
LOGIT_BIAS = -2.0
EPSILON = 1e-06

AXES = ("y_lo", "core", "x", "z", "y_hi")
SIZES = (2, 2, 4, 8, 2)
PLANE = ("y_lo", "y_hi", "x")
DEVS = 64
F32, BF16 = jnp.float32, jnp.bfloat16
VMEM, SMEM = pltpu.VMEM, pltpu.SMEM


def moved(block, flip, shift):
    pairs = []
    for source in range(4 * DEVS):
        group, dev = divmod(source, DEVS)
        pairs.append((source, (group ^ flip) * DEVS + (dev + shift) % DEVS))
    return lax.ppermute(block, AXES, pairs)


def dot(a, b, contract):
    return lax.dot_general(a, b, (contract, ((), ())), preferred_element_type=F32)


PLAIN, ROWS, COLUMNS = ((1,), (0,)), ((1,), (1,)), ((0,), (0,))


def project(inputs, weight):
    projected = dot(inputs, weight, PLAIN)
    inverse = lax.rsqrt(jnp.sum(projected * projected, axis=-1, keepdims=True) + EPSILON)
    return (projected * inverse, inverse)


def direction(grad, unit, inverse):
    inner = jnp.sum(unit * grad, axis=-1, keepdims=True)
    return ((grad - unit * inner) * inverse).astype(BF16)


def pair_weights(docids, queries, labels, doc_start):
    logits = LOGIT_SCALE * dot(docids, queries, ROWS) + LOGIT_BIAS
    rows = doc_start + lax.broadcasted_iota(jnp.int32, logits.shape, 0)
    return (jax.nn.sigmoid(logits) - jnp.where(labels == rows, 1.0, 0.0)).astype(BF16)


def own_kernel(starts, queries, docids, labels, head_query, head_docid,
               docid_vec, docid_unit, docid_inverse, docid_grad, query_head):
    unit, inverse = project(docids[...], head_docid[...])
    docid_unit[...] = unit
    docid_inverse[...] = inverse
    docid_vec[...] = unit.astype(BF16)
    unit, inverse = project(queries[...], head_query[...])
    query_vec = unit.astype(BF16)
    weights = pair_weights(docid_vec[...], query_vec, labels[...], starts[0])
    docid_grad[...] = LOGIT_SCALE * dot(weights, query_vec, PLAIN)
    query_grad = LOGIT_SCALE * dot(weights, docid_vec[...], COLUMNS)
    query_head[...] = dot(queries[...], direction(query_grad, unit, inverse), COLUMNS)


def project_kernel(docids, head_docid, docid_vec, docid_unit, docid_inverse):
    unit, inverse = project(docids[...], head_docid[...])
    docid_unit[...] = unit
    docid_inverse[...] = inverse
    docid_vec[...] = unit.astype(BF16)


def pair(starts, queries, labels, head_query, docid_vec, far_vec, docid_in, head_in):
    unit, inverse = project(queries[...], head_query[...])
    query_vec = unit.astype(BF16)
    weights = pair_weights(far_vec[...], query_vec, labels[...], starts[1])
    far_grad = LOGIT_SCALE * dot(weights, query_vec, PLAIN)
    query_grad = dot(weights, far_vec[...], COLUMNS)
    weights = pair_weights(docid_vec[...], query_vec, labels[...], starts[0])
    docid_grad = docid_in[...] + LOGIT_SCALE * dot(weights, query_vec, PLAIN)
    query_grad = LOGIT_SCALE * (query_grad + dot(weights, docid_vec[...], COLUMNS))
    head = head_in[...] + dot(queries[...], direction(query_grad, unit, inverse), COLUMNS)
    return docid_grad, far_grad, head


def pair_kernel(*refs):
    ins, outs = refs[:8], refs[8:]
    for out, value in zip(outs, pair(*ins), strict=True):
        out[...] = value


def last_kernel(starts, queries, labels, head_query, docid_vec, far_vec, docid_in, head_in, far_in,
                docids, docid_unit, docid_inverse, far, far_unit, far_inverse,
                docid_out, far_sent, kept, sent):
    docid_grad, far_grad, query = pair(
        starts, queries, labels, head_query, docid_vec, far_vec, docid_in, head_in
    )
    far_grad = far_grad + far_in[...]
    docid_out[...] = docid_grad
    far_sent[...] = far_grad.astype(BF16)
    head = dot(docids[...], direction(docid_grad, docid_unit[...], docid_inverse[...]), COLUMNS)
    head = head + dot(far[...], direction(far_grad, far_unit[...], far_inverse[...]), COLUMNS)
    mine = jnp.zeros(head.shape, jnp.int32) + starts[2] == 0
    kept[...] = jnp.where(mine, query, head)
    sent[...] = jnp.where(mine, head, query).astype(BF16)


def update_kernel(docid_grad, back, docid_unit, docid_inverse, head_docid, update):
    grad = docid_grad[...] + back[...].astype(F32)
    direct = direction(grad, docid_unit[...], docid_inverse[...])
    grad = dot(direct, head_docid[...], ROWS)
    scale = lax.rsqrt(jnp.mean(grad * grad, axis=-1, keepdims=True) + EPSILON)
    update[...] = (grad * scale).astype(BF16)


def unit_rms(grad):
    return grad * lax.rsqrt(jnp.sum(grad * grad) / (grad.shape[0] * grad.shape[1]) + EPSILON)


def step_kernel(starts, mine, other, query_step, docid_step):
    mine_step = unit_rms(mine[...].astype(F32))
    other_step = unit_rms(other[...].astype(F32))
    here = jnp.zeros(mine_step.shape, jnp.int32) + starts[2] == 0
    query_step[...] = jnp.where(here, mine_step, other_step)
    docid_step[...] = jnp.where(here, other_step, mine_step)


def call(kernel, outs, *args, flops=0, scalars=True):
    specs = [pl.BlockSpec(memory_space=VMEM) for _ in args]
    if scalars:
        specs[0] = pl.BlockSpec(memory_space=SMEM)
    moved_bytes = sum(a.size * a.dtype.itemsize for a in args)
    moved_bytes += sum(o.size * o.dtype.itemsize for o in outs)
    return pl.pallas_call(
        kernel,
        out_shape=outs,
        in_specs=specs,
        out_specs=[pl.BlockSpec(memory_space=VMEM) for _ in outs],
        compiler_params=pltpu.CompilerParams(vmem_limit_bytes=20 * 2**20),
        cost_estimate=pl.CostEstimate(flops=flops, transcendentals=0, bytes_accessed=moved_bytes),
    )(*args)


def total(kept, sent, back):
    rows, width = kept.shape
    value = kept + moved(sent, 1, 0).astype(F32)
    plane, line = SIZES[0] * SIZES[2] * SIZES[4], SIZES[3]
    piece = value.astype(BF16).reshape(plane, rows // plane, width)
    piece = lax.all_to_all(piece, PLANE, 0, 0, tiled=True)
    piece = jnp.sum(piece.astype(F32), axis=0).astype(BF16)
    piece, back = lax.optimization_barrier((piece, back))
    piece = jnp.broadcast_to(piece[None], (line,) + piece.shape)
    piece = lax.all_to_all(piece, "z", 0, 0, tiled=True)
    piece = jnp.sum(piece.astype(F32), axis=0).astype(BF16)
    piece = jnp.broadcast_to(piece[None], (plane,) + piece.shape)
    mine = lax.all_to_all(piece, PLANE, 0, 0, tiled=True).reshape(rows, width)
    return mine, moved(mine, 1, 0), back


def per_device(queries, docids, labels, head_query, head_docid):
    rows, width = queries.shape
    side = head_query.shape[1]
    core = lax.axis_index("core")
    group = lax.axis_index("y_lo") * 2 + core
    dev = (lax.axis_index("x") * 8 + lax.axis_index("z")) * 2 + lax.axis_index("y_hi")
    own_start = (group * DEVS + dev) * rows
    far_start = (group * DEVS + (dev - 2) % DEVS) * rows
    starts = jnp.stack([own_start, far_start, core]).astype(jnp.int32)

    queries_2, labels_2 = moved(queries, 2, -2), moved(labels, 2, -2)
    far = moved(docids, 0, 2)
    queries_1, labels_1 = moved(queries, 1, -1), moved(labels, 1, -1)

    def out(shape, dtype=F32):
        return jax.ShapeDtypeStruct(shape, dtype)

    block, column, head = (rows, side), (rows, 1), (width, side)
    mul = 2 * rows * width * side
    pair_flops = 2 * rows * rows * side
    docid_vec, docid_unit, docid_inverse, docid_grad, query_head = call(
        own_kernel,
        [out(block, BF16), out(block), out(column), out(block), out(head)],
        starts, queries, docids, labels[None], head_query, head_docid,
        flops=3 * mul + 3 * pair_flops,
    )
    far_vec, far_unit, far_inverse = call(
        project_kernel,
        [out(block, BF16), out(block), out(column)],
        far, head_docid,
        flops=mul, scalars=False,
    )
    docid_grad, far_grad, query_head = call(
        pair_kernel,
        [out(block), out(block), out(head)],
        starts, queries_2, labels_2[None], head_query, docid_vec, far_vec, docid_grad, query_head,
        flops=2 * mul + 6 * pair_flops,
    )
    queries_1, labels_1, far_grad = lax.optimization_barrier((queries_1, labels_1, far_grad))
    docid_grad, far_sent, kept, sent = call(
        last_kernel,
        [out(block), out(block, BF16), out(head), out(head, BF16)],
        starts, queries_1, labels_1[None], head_query, docid_vec, far_vec, docid_grad, query_head, far_grad,
        docids, docid_unit, docid_inverse, far, far_unit, far_inverse,
        flops=4 * mul + 6 * pair_flops,
    )
    back = moved(far_sent, 0, -2)
    mine, other, back = total(kept, sent, back)
    (doc_update,) = call(
        update_kernel,
        [out((rows, width), BF16)],
        docid_grad, back, docid_unit, docid_inverse, head_docid,
        flops=mul, scalars=False,
    )
    query_step, docid_step = call(step_kernel, [out(head), out(head)], starts, mine, other)
    return (doc_update, query_step, docid_step)


def solution(mesh):
    split = Mesh(mesh.devices.reshape(SIZES), AXES)
    rows = P(AXES)
    return jax.shard_map(
        per_device,
        mesh=split,
        in_specs=(rows, rows, rows, P(), P()),
        out_specs=(rows, P(), P()),
        check_vma=False,
    )
```

```python
import functools

import jax
import jax.numpy as jnp
from jax import lax
from jax.experimental import pallas as pl
from jax.experimental.pallas import tpu as pltpu
from jax.sharding import Mesh
from jax.sharding import PartitionSpec as P

LOGIT_SCALE = 5.0
LOGIT_BIAS = -2.0
EPSILON = 1e-06

AXES = ("y_lo", "core", "x", "z", "y_hi")
SIZES = (2, 2, 4, 8, 2)
PLANE = ("y_lo", "y_hi", "x")
DEVS = 64
F32, BF16 = jnp.float32, jnp.bfloat16
VMEM, SMEM = pltpu.VMEM, pltpu.SMEM


def moved(block, flip, shift):
    pairs = []
    for source in range(4 * DEVS):
        group, dev = divmod(source, DEVS)
        pairs.append((source, (group ^ flip) * DEVS + (dev + shift) % DEVS))
    return lax.ppermute(block, AXES, pairs)


def dot(a, b, contract):
    return lax.dot_general(a, b, (contract, ((), ())), preferred_element_type=F32)


PLAIN, ROWS, COLUMNS = ((1,), (0,)), ((1,), (1,)), ((0,), (0,))


def project(inputs, weight):
    projected = dot(inputs, weight, PLAIN)
    inverse = lax.rsqrt(jnp.sum(projected * projected, axis=-1, keepdims=True) + EPSILON)
    return (projected * inverse, inverse)


def direction(grad, unit, scale):
    inner = jnp.sum(unit * grad, axis=-1, keepdims=True)
    return ((grad - unit * inner) * scale).astype(BF16)


def pair_weights(docids, queries, labels, doc_start):
    logits = LOGIT_SCALE * dot(docids, queries, ROWS) + LOGIT_BIAS
    rows = doc_start + lax.broadcasted_iota(jnp.int32, logits.shape, 0)
    return (jax.nn.sigmoid(logits) - jnp.where(labels == rows, 1.0, 0.0)).astype(BF16)


def pack_kernel(start, labels, queries, packed):
    count = packed.shape[0] - 16
    packed[0:count, :] = queries[start : start + count, :]
    label = labels[:, start : start + count]
    row = lax.broadcasted_iota(jnp.int32, (16, count), 0)
    digit = jnp.where(row == 0, label & 63, jnp.where(row == 1, (label >> 6) & 63, label >> 12))
    packed[count : count + 16, :] = jnp.zeros((16, packed.shape[1]), BF16)
    packed[count : count + 16, 0:count] = jnp.where(row < 3, digit, 0).astype(F32).astype(BF16)


def pack(labels, queries, start, count):
    (packed,) = call(
        functools.partial(pack_kernel, start),
        [jax.ShapeDtypeStruct((count + 16, queries.shape[1]), BF16)],
        labels, queries,
        scalars=False,
    )
    return packed


def unpacked(part):
    count = part.shape[0] - 16
    digits = part[count : count + 16, 0:count].astype(F32)
    labels = digits[0:1] + 64.0 * digits[1:2] + 4096.0 * digits[2:3]
    return part[0:count, :], labels.astype(jnp.int32)


def own_kernel(starts, labels, queries, docids, head_query, head_docid,
               docid_vec, docid_unit, docid_scale, docid_grad, query_head):
    unit, inverse = project(docids[...], head_docid[...])
    docid_unit[...] = unit
    docid_scale[...] = LOGIT_SCALE * inverse
    vec = unit.astype(BF16)
    docid_vec[...] = vec
    unit, inverse = project(queries[...], head_query[...])
    query_vec = unit.astype(BF16)
    weights = pair_weights(vec, query_vec, labels[...], starts[0])
    docid_grad[...] = dot(weights, query_vec, PLAIN)
    query_grad = dot(weights, vec, COLUMNS)
    query_head[...] = dot(queries[...], direction(query_grad, unit, LOGIT_SCALE * inverse), COLUMNS)


def pair(starts, part, head_query, docid_vec, far_vec):
    queries, labels = unpacked(part)
    unit, inverse = project(queries, head_query[...])
    query_vec = unit.astype(BF16)
    weights = pair_weights(far_vec, query_vec, labels, starts[1])
    far_grad = dot(weights, query_vec, PLAIN)
    query_grad = dot(weights, far_vec, COLUMNS)
    weights = pair_weights(docid_vec, query_vec, labels, starts[0])
    docid_grad = dot(weights, query_vec, PLAIN)
    query_grad = query_grad + dot(weights, docid_vec, COLUMNS)
    head = dot(queries, direction(query_grad, unit, LOGIT_SCALE * inverse), COLUMNS)
    return docid_grad, far_grad, head


def first_kernel(starts, part, head_query, docid_vec, docid_in, head_in, far, head_docid,
                 docid_out, far_out, head_out, far_vec, far_unit, far_scale):
    unit, inverse = project(far[...], head_docid[...])
    far_unit[...] = unit
    far_scale[...] = LOGIT_SCALE * inverse
    vec = unit.astype(BF16)
    far_vec[...] = vec
    docid_grad, far_out[...], head = pair(starts, part, head_query, docid_vec[...], vec)
    docid_out[...] = docid_in[...] + docid_grad
    head_out[...] = head_in[...] + head


def next_kernel(starts, part, head_query, docid_vec, docid_in, head_in, far_vec, far_in,
                docid_out, far_out, head_out):
    docid_grad, far_grad, head = pair(starts, part, head_query, docid_vec[...], far_vec[...])
    docid_out[...] = docid_in[...] + docid_grad
    far_out[...] = far_in[...] + far_grad
    head_out[...] = head_in[...] + head


def last_kernel(starts, part, head_query, docid_vec, docid_in, head_in, far_vec, far_in,
                docids, docid_unit, docid_scale, far, far_unit, far_scale,
                docid_out, far_sent, kept, sent):
    docid_grad, far_grad, query = pair(starts, part, head_query, docid_vec[...], far_vec[...])
    docid_grad = docid_grad + docid_in[...]
    far_grad = far_grad + far_in[...]
    query = query + head_in[...]
    docid_out[...] = docid_grad
    far_sent[...] = far_grad.astype(BF16)
    head = dot(docids[...], direction(docid_grad, docid_unit[...], docid_scale[...]), COLUMNS)
    head = head + dot(far[...], direction(far_grad, far_unit[...], far_scale[...]), COLUMNS)
    mine = jnp.zeros(head.shape, jnp.int32) + starts[2] == 0
    kept[...] = jnp.where(mine, query, head)
    sent[...] = jnp.where(mine, head, query).astype(BF16)


def update_kernel(docid_grad, back, docid_unit, docid_scale, head_docid, update):
    grad = docid_grad[...] + back[...].astype(F32)
    direct = direction(grad, docid_unit[...], docid_scale[...])
    grad = dot(direct, head_docid[...], ROWS)
    scale = lax.rsqrt(jnp.mean(grad * grad, axis=-1, keepdims=True) + EPSILON)
    update[...] = (grad * scale).astype(BF16)


def rms_scale(grad):
    grad = grad.astype(F32)
    return lax.rsqrt(jnp.sum(grad * grad) / (grad.shape[0] * grad.shape[1]) + EPSILON)


def write(head, target, staged, sems):
    depth, block = staged.shape[0], staged.shape[1]
    scale = rms_scale(head[...])
    copies = []
    for step in range(depth):
        rows = slice(step * block, (step + 1) * block)
        staged[step] = head[rows, :].astype(F32) * scale
        copies.append(pltpu.make_async_copy(staged.at[step], target.at[rows], sems.at[step]))
        copies[-1].start()
    for copy in copies:
        copy.wait()


def mine_kernel(starts, mine, query_step, docid_step, staged, sems):
    @pl.when(starts[2] == 0)
    def _():
        write(mine, query_step, staged, sems)

    @pl.when(starts[2] != 0)
    def _():
        write(mine, docid_step, staged, sems)


def other_kernel(starts, other, query_in, docid_in, query_step, docid_step, staged, sems):
    del query_in, docid_in

    @pl.when(starts[2] == 0)
    def _():
        write(other, docid_step, staged, sems)

    @pl.when(starts[2] != 0)
    def _():
        write(other, query_step, staged, sems)


def steps(starts, mine, other):
    rows, width = mine.shape
    depth = 3
    outside = pl.BlockSpec(memory_space=pltpu.HBM)
    common = dict(
        out_shape=[jax.ShapeDtypeStruct((rows, width), F32)] * 2,
        out_specs=[outside] * 2,
        scratch_shapes=[VMEM((depth, rows // depth, width), F32), pltpu.SemaphoreType.DMA((depth,))],
        compiler_params=pltpu.CompilerParams(vmem_limit_bytes=24 * 2**20),
    )
    given = [pl.BlockSpec(memory_space=SMEM), pl.BlockSpec(memory_space=VMEM)]
    written = pl.pallas_call(mine_kernel, in_specs=given, **common)(starts, mine)
    return pl.pallas_call(
        other_kernel, in_specs=given + [outside] * 2, input_output_aliases={2: 0, 3: 1}, **common
    )(starts, other, *written)


def call(kernel, outs, *args, flops=0, scalars=True):
    specs = [pl.BlockSpec(memory_space=VMEM) for _ in args]
    if scalars:
        specs[0] = pl.BlockSpec(memory_space=SMEM)
    moved_bytes = sum(a.size * a.dtype.itemsize for a in args)
    moved_bytes += sum(o.size * o.dtype.itemsize for o in outs)
    return pl.pallas_call(
        kernel,
        out_shape=outs,
        in_specs=specs,
        out_specs=[pl.BlockSpec(memory_space=VMEM) for _ in outs],
        compiler_params=pltpu.CompilerParams(vmem_limit_bytes=20 * 2**20),
        cost_estimate=pl.CostEstimate(flops=flops, transcendentals=0, bytes_accessed=moved_bytes),
    )(*args)


def total(kept, sent, update):
    rows, width = kept.shape
    value = kept + moved(sent, 1, 0).astype(F32)
    plane, line = SIZES[0] * SIZES[2] * SIZES[4], SIZES[3]
    for axes, size in ((PLANE[:2], SIZES[0] * SIZES[4]), (PLANE[2], SIZES[2])):
        piece = value.astype(BF16).reshape(size, -1, width)
        piece = lax.all_to_all(piece, axes, 0, 0, tiled=True)
        value = jnp.sum(piece.astype(F32), axis=0)
    piece = value.astype(BF16)
    piece, update = lax.optimization_barrier((piece, update))
    piece = piece.reshape(line, -1, 128)
    piece = lax.all_to_all(piece, "z", 0, 0, tiled=True)
    piece = jnp.sum(piece.astype(F32), axis=0).astype(BF16)
    piece = jnp.broadcast_to(piece[None], (line,) + piece.shape)
    piece = lax.all_to_all(piece, "z", 0, 0, tiled=True).reshape(rows // plane, width)
    piece = jnp.broadcast_to(piece[None], (plane,) + piece.shape)
    mine = lax.all_to_all(piece, PLANE, 0, 0, tiled=True).reshape(rows, width)
    return mine, moved(mine, 1, 0), update


def per_device(queries, docids, labels, head_query, head_docid):
    rows, width = queries.shape
    side = head_query.shape[1]
    core = lax.axis_index("core")
    group = lax.axis_index("y_lo") * 2 + core
    dev = (lax.axis_index("x") * 8 + lax.axis_index("z")) * 2 + lax.axis_index("y_hi")
    own_start = (group * DEVS + dev) * rows
    far_start = (group * DEVS + (dev - 2) % DEVS) * rows
    starts = jnp.stack([own_start, far_start, core]).astype(jnp.int32)

    far = moved(docids, 0, 2)
    cut = 384
    row = labels[None]
    whole = pack(row, queries, 0, rows)
    queries_2 = moved(whole, 2, -2)
    rest, whole = lax.optimization_barrier((queries, whole))
    part_a = pack(row, rest, 0, cut)
    queries_1a = moved(part_a, 1, -1)
    rest, part_a = lax.optimization_barrier((rest, part_a))
    queries_1b = moved(pack(row, rest, cut, rows - cut), 1, -1)

    def out(shape, dtype=F32):
        return jax.ShapeDtypeStruct(shape, dtype)

    block, column, head = (rows, side), (rows, 1), (width, side)
    mul = 2 * rows * width * side
    pair_flops = 2 * rows * rows * side
    docid_vec, docid_unit, docid_scale, docid_grad, query_head = call(
        own_kernel,
        [out(block, BF16), out(block), out(column), out(block), out(head)],
        starts, row, queries, docids, head_query, head_docid,
        flops=3 * mul + 3 * pair_flops,
    )
    docid_grad, far_grad, query_head, far_vec, far_unit, far_scale = call(
        first_kernel,
        [out(block), out(block), out(head), out(block, BF16), out(block), out(column)],
        starts, queries_2, head_query, docid_vec, docid_grad, query_head, far, head_docid,
        flops=3 * mul + 6 * pair_flops,
    )
    queries_1a, far_grad = lax.optimization_barrier((queries_1a, far_grad))
    docid_grad, far_grad, query_head = call(
        next_kernel,
        [out(block), out(block), out(head)],
        starts, queries_1a, head_query, docid_vec, docid_grad, query_head, far_vec, far_grad,
        flops=mul + 4 * pair_flops,
    )
    queries_1b, far_grad = lax.optimization_barrier((queries_1b, far_grad))
    docid_grad, far_sent, kept, sent = call(
        last_kernel,
        [out(block), out(block, BF16), out(head), out(head, BF16)],
        starts, queries_1b, head_query, docid_vec, docid_grad, query_head, far_vec, far_grad,
        docids, docid_unit, docid_scale, far, far_unit, far_scale,
        flops=3 * mul + 4 * pair_flops,
    )
    back = moved(far_sent, 0, -2)
    (doc_update,) = call(
        update_kernel,
        [out((rows, width), BF16)],
        docid_grad, back, docid_unit, docid_scale, head_docid,
        flops=40 * mul, scalars=False,
    )
    mine, other, doc_update = total(kept, sent, doc_update)
    query_step, docid_step = steps(starts, mine, other)
    return (doc_update, query_step, docid_step)


def solution(mesh):
    split = Mesh(mesh.devices.reshape(SIZES), AXES)
    rows = P(AXES)
    return jax.shard_map(
        per_device,
        mesh=split,
        in_specs=(rows, rows, rows, P(), P()),
        out_specs=(rows, P(), P()),
        check_vma=False,
    )
```

```python
import functools

import jax
import jax.numpy as jnp
from jax import lax
from jax.experimental import pallas as pl
from jax.experimental.pallas import tpu as pltpu
from jax.sharding import Mesh
from jax.sharding import PartitionSpec as P

LOGIT_SCALE = 5.0
LOGIT_BIAS = -2.0
EPSILON = 1e-06

AXES = ("y_lo", "core", "x", "z", "y_hi")
SIZES = (2, 2, 4, 8, 2)
PLANE = ("y_lo", "y_hi", "x")
DEVS = 64
F32, BF16 = jnp.float32, jnp.bfloat16
VMEM, SMEM = pltpu.VMEM, pltpu.SMEM


def moved(block, flip, shift):
    pairs = []
    for source in range(4 * DEVS):
        group, dev = divmod(source, DEVS)
        pairs.append((source, (group ^ flip) * DEVS + (dev + shift) % DEVS))
    return lax.ppermute(block, AXES, pairs)


def dot(a, b, contract):
    return lax.dot_general(a, b, (contract, ((), ())), preferred_element_type=F32)


PLAIN, ROWS, COLUMNS = ((1,), (0,)), ((1,), (1,)), ((0,), (0,))


def project(inputs, weight):
    projected = dot(inputs, weight, PLAIN)
    inverse = lax.rsqrt(jnp.sum(projected * projected, axis=-1, keepdims=True) + EPSILON)
    return (projected * inverse, inverse)


def direction(grad, unit, scale):
    inner = jnp.sum(unit * grad, axis=-1, keepdims=True)
    return ((grad - unit * inner) * scale).astype(BF16)


def pair_weights(docids, queries, labels, doc_start):
    logits = LOGIT_SCALE * dot(docids, queries, ROWS) + LOGIT_BIAS
    rows = doc_start + lax.broadcasted_iota(jnp.int32, logits.shape, 0)
    return (jax.nn.sigmoid(logits) - jnp.where(labels == rows, 1.0, 0.0)).astype(BF16)


def pack_kernel(start, labels, queries, packed):
    count = packed.shape[0] - 16
    packed[0:count, :] = queries[start : start + count, :]
    label = labels[:, start : start + count]
    row = lax.broadcasted_iota(jnp.int32, (16, count), 0)
    digit = jnp.where(row == 0, label & 63, jnp.where(row == 1, (label >> 6) & 63, label >> 12))
    packed[count : count + 16, :] = jnp.zeros((16, packed.shape[1]), BF16)
    packed[count : count + 16, 0:count] = jnp.where(row < 3, digit, 0).astype(F32).astype(BF16)


def pack(labels, queries, start, count):
    (packed,) = call(
        functools.partial(pack_kernel, start),
        [jax.ShapeDtypeStruct((count + 16, queries.shape[1]), BF16)],
        labels, queries,
        scalars=False,
    )
    return packed


def unpacked(part):
    count = part.shape[0] - 16
    digits = part[count : count + 16, 0:count].astype(F32)
    labels = digits[0:1] + 64.0 * digits[1:2] + 4096.0 * digits[2:3]
    return part[0:count, :], labels.astype(jnp.int32)


def own_kernel(starts, labels, queries, docids, head_query, head_docid,
               docid_vec, docid_unit, docid_scale, docid_grad, query_head):
    unit, inverse = project(docids[...], head_docid[...])
    docid_unit[...] = unit
    docid_scale[...] = LOGIT_SCALE * inverse
    vec = unit.astype(BF16)
    docid_vec[...] = vec
    unit, inverse = project(queries[...], head_query[...])
    query_vec = unit.astype(BF16)
    weights = pair_weights(vec, query_vec, labels[...], starts[0])
    docid_grad[...] = dot(weights, query_vec, PLAIN)
    query_grad = dot(weights, vec, COLUMNS)
    query_head[...] = dot(queries[...], direction(query_grad, unit, LOGIT_SCALE * inverse), COLUMNS)


def pair(starts, queries, labels, head_query, docid_vec, far_vec):
    unit, inverse = project(queries, head_query[...])
    query_vec = unit.astype(BF16)
    weights = pair_weights(far_vec, query_vec, labels, starts[1])
    far_grad = dot(weights, query_vec, PLAIN)
    query_grad = dot(weights, far_vec, COLUMNS)
    weights = pair_weights(docid_vec, query_vec, labels, starts[0])
    docid_grad = dot(weights, query_vec, PLAIN)
    query_grad = query_grad + dot(weights, docid_vec, COLUMNS)
    head = dot(queries, direction(query_grad, unit, LOGIT_SCALE * inverse), COLUMNS)
    return docid_grad, far_grad, head


def first_kernel(starts, queries, labels, head_query, docid_vec, docid_in, head_in, far, head_docid,
                 docid_out, far_out, head_out, far_vec, far_unit, far_scale):
    unit, inverse = project(far[...], head_docid[...])
    far_unit[...] = unit
    far_scale[...] = LOGIT_SCALE * inverse
    vec = unit.astype(BF16)
    far_vec[...] = vec
    docid_grad, far_out[...], head = pair(starts, queries[...], labels[...], head_query, docid_vec[...], vec)
    docid_out[...] = docid_in[...] + docid_grad
    head_out[...] = head_in[...] + head


def next_kernel(starts, part, head_query, docid_vec, docid_in, head_in, far_vec, far_in,
                docid_out, far_out, head_out):
    docid_grad, far_grad, head = pair(starts, *unpacked(part), head_query, docid_vec[...], far_vec[...])
    docid_out[...] = docid_in[...] + docid_grad
    far_out[...] = far_in[...] + far_grad
    head_out[...] = head_in[...] + head


def last_kernel(starts, part, head_query, docid_vec, docid_in, head_in, far_vec, far_in,
                docids, docid_unit, docid_scale, far, far_unit, far_scale,
                docid_out, far_sent, kept, sent):
    docid_grad, far_grad, query = pair(starts, *unpacked(part), head_query, docid_vec[...], far_vec[...])
    docid_grad = docid_grad + docid_in[...]
    far_grad = far_grad + far_in[...]
    query = query + head_in[...]
    docid_out[...] = docid_grad
    far_sent[...] = far_grad.astype(BF16)
    head = dot(docids[...], direction(docid_grad, docid_unit[...], docid_scale[...]), COLUMNS)
    head = head + dot(far[...], direction(far_grad, far_unit[...], far_scale[...]), COLUMNS)
    mine = jnp.zeros(head.shape, jnp.int32) + starts[2] == 0
    kept[...] = jnp.where(mine, query, head)
    sent[...] = jnp.where(mine, head, query).astype(BF16)


def update_kernel(docid_grad, back, docid_unit, docid_scale, head_docid, update):
    grad = docid_grad[...] + back[...].astype(F32)
    direct = direction(grad, docid_unit[...], docid_scale[...])
    grad = dot(direct, head_docid[...], ROWS)
    scale = lax.rsqrt(jnp.mean(grad * grad, axis=-1, keepdims=True) + EPSILON)
    update[...] = (grad * scale).astype(BF16)


def rms_scale(grad):
    grad = grad.astype(F32)
    return lax.rsqrt(jnp.sum(grad * grad) / (grad.shape[0] * grad.shape[1]) + EPSILON)


def write(head, target, staged, sems):
    depth, block = staged.shape[0], staged.shape[1]
    scale = rms_scale(head[...])
    copies = []
    for step in range(depth):
        rows = slice(step * block, (step + 1) * block)
        staged[step] = head[rows, :].astype(F32) * scale
        copies.append(pltpu.make_async_copy(staged.at[step], target.at[rows], sems.at[step]))
        copies[-1].start()
    for copy in copies:
        copy.wait()


def mine_kernel(starts, mine, query_step, docid_step, staged, sems):
    @pl.when(starts[2] == 0)
    def _():
        write(mine, query_step, staged, sems)

    @pl.when(starts[2] != 0)
    def _():
        write(mine, docid_step, staged, sems)


def other_kernel(starts, other, query_in, docid_in, query_step, docid_step, staged, sems):
    del query_in, docid_in

    @pl.when(starts[2] == 0)
    def _():
        write(other, docid_step, staged, sems)

    @pl.when(starts[2] != 0)
    def _():
        write(other, query_step, staged, sems)


def steps(starts, mine, other):
    rows, width = mine.shape
    depth = 3
    outside = pl.BlockSpec(memory_space=pltpu.HBM)
    common = dict(
        out_shape=[jax.ShapeDtypeStruct((rows, width), F32)] * 2,
        out_specs=[outside] * 2,
        scratch_shapes=[VMEM((depth, rows // depth, width), F32), pltpu.SemaphoreType.DMA((depth,))],
        compiler_params=pltpu.CompilerParams(vmem_limit_bytes=24 * 2**20),
    )
    given = [pl.BlockSpec(memory_space=SMEM), pl.BlockSpec(memory_space=VMEM)]
    written = pl.pallas_call(mine_kernel, in_specs=given, **common)(starts, mine)
    return pl.pallas_call(
        other_kernel, in_specs=given + [outside] * 2, input_output_aliases={2: 0, 3: 1}, **common
    )(starts, other, *written)


def call(kernel, outs, *args, flops=0, scalars=True):
    specs = [pl.BlockSpec(memory_space=VMEM) for _ in args]
    if scalars:
        specs[0] = pl.BlockSpec(memory_space=SMEM)
    moved_bytes = sum(a.size * a.dtype.itemsize for a in args)
    moved_bytes += sum(o.size * o.dtype.itemsize for o in outs)
    return pl.pallas_call(
        kernel,
        out_shape=outs,
        in_specs=specs,
        out_specs=[pl.BlockSpec(memory_space=VMEM) for _ in outs],
        compiler_params=pltpu.CompilerParams(vmem_limit_bytes=20 * 2**20),
        cost_estimate=pl.CostEstimate(flops=flops, transcendentals=0, bytes_accessed=moved_bytes),
    )(*args)


def total(kept, sent, update):
    rows, width = kept.shape
    value = kept + moved(sent, 1, 0).astype(F32)
    plane, line = SIZES[0] * SIZES[2] * SIZES[4], SIZES[3]
    piece = value.astype(BF16).reshape(SIZES[0] * SIZES[4], -1, width)
    piece = lax.all_to_all(piece, PLANE[:2], 0, 0, tiled=True)
    piece = jnp.sum(piece.astype(F32), axis=0).astype(BF16)
    piece = piece.reshape(SIZES[2] * line, -1, 128)
    piece = lax.all_to_all(piece, ("x", "z"), 0, 0, tiled=True)
    piece = jnp.sum(piece.astype(F32), axis=0).astype(BF16)
    piece, update = lax.optimization_barrier((piece, update))
    piece = jnp.broadcast_to(piece[None], (line,) + piece.shape)
    piece = lax.all_to_all(piece, "z", 0, 0, tiled=True).reshape(rows // plane, width)
    piece = jnp.broadcast_to(piece[None], (plane,) + piece.shape)
    mine = lax.all_to_all(piece, PLANE, 0, 0, tiled=True).reshape(rows, width)
    return mine, moved(mine, 1, 0), update


def per_device(queries, docids, labels, head_query, head_docid):
    rows, width = queries.shape
    side = head_query.shape[1]
    core = lax.axis_index("core")
    group = lax.axis_index("y_lo") * 2 + core
    dev = (lax.axis_index("x") * 8 + lax.axis_index("z")) * 2 + lax.axis_index("y_hi")
    own_start = (group * DEVS + dev) * rows
    far_start = (group * DEVS + (dev - 2) % DEVS) * rows
    starts = jnp.stack([own_start, far_start, core]).astype(jnp.int32)

    far = moved(docids, 0, 2)
    cut = 384
    row = labels[None]
    queries_2, labels_2 = moved(queries, 2, -2), moved(labels, 2, -2)
    part_a = pack(row, queries, 0, cut)
    queries_1a = moved(part_a, 1, -1)
    rest, part_a = lax.optimization_barrier((queries, part_a))
    queries_1b = moved(pack(row, rest, cut, rows - cut), 1, -1)

    def out(shape, dtype=F32):
        return jax.ShapeDtypeStruct(shape, dtype)

    block, column, head = (rows, side), (rows, 1), (width, side)
    mul = 2 * rows * width * side
    pair_flops = 2 * rows * rows * side
    docid_vec, docid_unit, docid_scale, docid_grad, query_head = call(
        own_kernel,
        [out(block, BF16), out(block), out(column), out(block), out(head)],
        starts, row, queries, docids, head_query, head_docid,
        flops=3 * mul + 3 * pair_flops,
    )
    docid_grad, far_grad, query_head, far_vec, far_unit, far_scale = call(
        first_kernel,
        [out(block), out(block), out(head), out(block, BF16), out(block), out(column)],
        starts, queries_2, labels_2[None], head_query, docid_vec, docid_grad, query_head, far, head_docid,
        flops=3 * mul + 6 * pair_flops,
    )
    queries_1a, far_grad = lax.optimization_barrier((queries_1a, far_grad))
    docid_grad, far_grad, query_head = call(
        next_kernel,
        [out(block), out(block), out(head)],
        starts, queries_1a, head_query, docid_vec, docid_grad, query_head, far_vec, far_grad,
        flops=mul + 4 * pair_flops,
    )
    queries_1b, far_grad = lax.optimization_barrier((queries_1b, far_grad))
    docid_grad, far_sent, kept, sent = call(
        last_kernel,
        [out(block), out(block, BF16), out(head), out(head, BF16)],
        starts, queries_1b, head_query, docid_vec, docid_grad, query_head, far_vec, far_grad,
        docids, docid_unit, docid_scale, far, far_unit, far_scale,
        flops=3 * mul + 4 * pair_flops,
    )
    back = moved(far_sent, 0, -2)
    (doc_update,) = call(
        update_kernel,
        [out((rows, width), BF16)],
        docid_grad, back, docid_unit, docid_scale, head_docid,
        flops=40 * mul, scalars=False,
    )
    mine, other, doc_update = total(kept, sent, doc_update)
    query_step, docid_step = steps(starts, mine, other)
    return (doc_update, query_step, docid_step)


def solution(mesh):
    split = Mesh(mesh.devices.reshape(SIZES), AXES)
    rows = P(AXES)
    return jax.shard_map(
        per_device,
        mesh=split,
        in_specs=(rows, rows, rows, P(), P()),
        out_specs=(rows, P(), P()),
        check_vma=False,
    )
```

```python
import functools

import jax
import jax.numpy as jnp
from jax import lax
from jax.experimental import pallas as pl
from jax.experimental.pallas import tpu as pltpu
from jax.sharding import Mesh
from jax.sharding import PartitionSpec as P

LOGIT_SCALE = 5.0
LOGIT_BIAS = -2.0
EPSILON = 1e-06

AXES = ("y_lo", "core", "x", "z", "y_hi")
SIZES = (2, 2, 4, 8, 2)
PLANE = ("y_lo", "y_hi", "x")
DEVS = 64
F32, BF16 = jnp.float32, jnp.bfloat16
VMEM, SMEM = pltpu.VMEM, pltpu.SMEM


def moved(block, flip, shift):
    pairs = []
    for source in range(4 * DEVS):
        group, dev = divmod(source, DEVS)
        pairs.append((source, (group ^ flip) * DEVS + (dev + shift) % DEVS))
    return lax.ppermute(block, AXES, pairs)


def dot(a, b, contract):
    return lax.dot_general(a, b, (contract, ((), ())), preferred_element_type=F32)


PLAIN, ROWS, COLUMNS = ((1,), (0,)), ((1,), (1,)), ((0,), (0,))


def project(inputs, weight):
    projected = dot(inputs, weight, PLAIN)
    inverse = lax.rsqrt(jnp.sum(projected * projected, axis=-1, keepdims=True) + EPSILON)
    return (projected * inverse, inverse)


def direction(grad, unit, scale):
    inner = jnp.sum(unit * grad, axis=-1, keepdims=True)
    return ((grad - unit * inner) * scale).astype(BF16)


def pair_weights(docids, queries, labels, doc_start):
    logits = LOGIT_SCALE * dot(docids, queries, ROWS) + LOGIT_BIAS
    rows = doc_start + lax.broadcasted_iota(jnp.int32, logits.shape, 0)
    return (jax.nn.sigmoid(logits) - jnp.where(labels == rows, 1.0, 0.0)).astype(BF16)


def pack_kernel(start, labels, queries, packed):
    count = packed.shape[0] - 16
    packed[0:count, :] = queries[start : start + count, :]
    label = labels[:, start : start + count]
    row = lax.broadcasted_iota(jnp.int32, (16, count), 0)
    digit = jnp.where(row == 0, label & 63, jnp.where(row == 1, (label >> 6) & 63, label >> 12))
    packed[count : count + 16, :] = jnp.zeros((16, packed.shape[1]), BF16)
    packed[count : count + 16, 0:count] = jnp.where(row < 3, digit, 0).astype(F32).astype(BF16)


def pack(labels, queries, start, count):
    (packed,) = call(
        functools.partial(pack_kernel, start),
        [jax.ShapeDtypeStruct((count + 16, queries.shape[1]), BF16)],
        labels, queries,
        scalars=False,
    )
    return packed


def unpacked(part):
    count = part.shape[0] - 16
    digits = part[count : count + 16, 0:count].astype(F32)
    labels = digits[0:1] + 64.0 * digits[1:2] + 4096.0 * digits[2:3]
    return part[0:count, :], labels.astype(jnp.int32)


def own_kernel(starts, labels, queries, docids, head_query, head_docid,
               docid_vec, docid_unit, docid_scale, docid_grad, query_head):
    unit, inverse = project(docids[...], head_docid[...])
    docid_unit[...] = unit
    docid_scale[...] = LOGIT_SCALE * inverse
    vec = unit.astype(BF16)
    docid_vec[...] = vec
    unit, inverse = project(queries[...], head_query[...])
    query_vec = unit.astype(BF16)
    weights = pair_weights(vec, query_vec, labels[...], starts[0])
    docid_grad[...] = dot(weights, query_vec, PLAIN)
    query_grad = dot(weights, vec, COLUMNS)
    query_head[...] = dot(queries[...], direction(query_grad, unit, LOGIT_SCALE * inverse), COLUMNS)


def query_kernel(queries, head_query, query_vec, query_unit, query_scale):
    unit, inverse = project(queries[...], head_query[...])
    query_unit[...] = unit
    query_scale[...] = LOGIT_SCALE * inverse
    query_vec[...] = unit.astype(BF16)


def scored(starts, queries, labels, query_vec, unit, scale, docid_vec, far_vec):
    weights = pair_weights(far_vec, query_vec, labels, starts[1])
    far_grad = dot(weights, query_vec, PLAIN)
    query_grad = dot(weights, far_vec, COLUMNS)
    weights = pair_weights(docid_vec, query_vec, labels, starts[0])
    docid_grad = dot(weights, query_vec, PLAIN)
    query_grad = query_grad + dot(weights, docid_vec, COLUMNS)
    head = dot(queries, direction(query_grad, unit, scale), COLUMNS)
    return docid_grad, far_grad, head


def pair(starts, queries, labels, head_query, docid_vec, far_vec):
    unit, inverse = project(queries, head_query[...])
    return scored(starts, queries, labels, unit.astype(BF16), unit, LOGIT_SCALE * inverse, docid_vec, far_vec)


def first_kernel(starts, queries, labels, query_vec, query_unit, query_scale, docid_vec, docid_in, head_in, far, head_docid,
                 docid_out, far_out, head_out, far_vec, far_unit, far_scale):
    unit, inverse = project(far[...], head_docid[...])
    far_unit[...] = unit
    far_scale[...] = LOGIT_SCALE * inverse
    vec = unit.astype(BF16)
    far_vec[...] = vec
    docid_grad, far_out[...], head = scored(
        starts, queries[...], labels[...], query_vec[...], query_unit[...], query_scale[...], docid_vec[...], vec
    )
    docid_out[...] = docid_in[...] + docid_grad
    head_out[...] = head_in[...] + head


def next_kernel(starts, part, head_query, docid_vec, docid_in, head_in, far_vec, far_in,
                docid_out, far_out, head_out):
    docid_grad, far_grad, head = pair(starts, *unpacked(part), head_query, docid_vec[...], far_vec[...])
    docid_out[...] = docid_in[...] + docid_grad
    far_out[...] = far_in[...] + far_grad
    head_out[...] = head_in[...] + head


def last_kernel(starts, part, head_query, docid_vec, docid_in, head_in, far_vec, far_in,
                docids, docid_unit, docid_scale, far, far_unit, far_scale,
                docid_out, far_sent, kept, sent):
    docid_grad, far_grad, query = pair(starts, *unpacked(part), head_query, docid_vec[...], far_vec[...])
    docid_grad = docid_grad + docid_in[...]
    far_grad = far_grad + far_in[...]
    query = query + head_in[...]
    docid_out[...] = docid_grad
    far_sent[...] = far_grad.astype(BF16)
    head = dot(docids[...], direction(docid_grad, docid_unit[...], docid_scale[...]), COLUMNS)
    head = head + dot(far[...], direction(far_grad, far_unit[...], far_scale[...]), COLUMNS)
    mine = jnp.zeros(head.shape, jnp.int32) + starts[2] == 0
    kept[...] = jnp.where(mine, query, head)
    sent[...] = jnp.where(mine, head, query).astype(BF16)


def update_kernel(docid_grad, back, docid_unit, docid_scale, head_docid, update):
    grad = docid_grad[...] + back[...].astype(F32)
    direct = direction(grad, docid_unit[...], docid_scale[...])
    grad = dot(direct, head_docid[...], ROWS)
    scale = lax.rsqrt(jnp.mean(grad * grad, axis=-1, keepdims=True) + EPSILON)
    update[...] = (grad * scale).astype(BF16)


def rms_scale(grad):
    grad = grad.astype(F32)
    return lax.rsqrt(jnp.sum(grad * grad) / (grad.shape[0] * grad.shape[1]) + EPSILON)


def write(head, target, staged, sems):
    depth, block = staged.shape[0], staged.shape[1]
    scale = rms_scale(head[...])
    copies = []
    for step in range(depth):
        rows = slice(step * block, (step + 1) * block)
        staged[step] = head[rows, :].astype(F32) * scale
        copies.append(pltpu.make_async_copy(staged.at[step], target.at[rows], sems.at[step]))
        copies[-1].start()
    for copy in copies:
        copy.wait()


def mine_kernel(starts, mine, query_step, docid_step, staged, sems):
    @pl.when(starts[2] == 0)
    def _():
        write(mine, query_step, staged, sems)

    @pl.when(starts[2] != 0)
    def _():
        write(mine, docid_step, staged, sems)


def other_kernel(starts, other, query_in, docid_in, query_step, docid_step, staged, sems):
    del query_in, docid_in

    @pl.when(starts[2] == 0)
    def _():
        write(other, docid_step, staged, sems)

    @pl.when(starts[2] != 0)
    def _():
        write(other, query_step, staged, sems)


def steps(starts, mine, other):
    rows, width = mine.shape
    depth = 3
    outside = pl.BlockSpec(memory_space=pltpu.HBM)
    common = dict(
        out_shape=[jax.ShapeDtypeStruct((rows, width), F32)] * 2,
        out_specs=[outside] * 2,
        scratch_shapes=[VMEM((depth, rows // depth, width), F32), pltpu.SemaphoreType.DMA((depth,))],
        compiler_params=pltpu.CompilerParams(vmem_limit_bytes=24 * 2**20),
    )
    given = [pl.BlockSpec(memory_space=SMEM), pl.BlockSpec(memory_space=VMEM)]
    written = pl.pallas_call(mine_kernel, in_specs=given, **common)(starts, mine)
    return pl.pallas_call(
        other_kernel, in_specs=given + [outside] * 2, input_output_aliases={2: 0, 3: 1}, **common
    )(starts, other, *written)


def call(kernel, outs, *args, flops=0, scalars=True):
    specs = [pl.BlockSpec(memory_space=VMEM) for _ in args]
    if scalars:
        specs[0] = pl.BlockSpec(memory_space=SMEM)
    moved_bytes = sum(a.size * a.dtype.itemsize for a in args)
    moved_bytes += sum(o.size * o.dtype.itemsize for o in outs)
    return pl.pallas_call(
        kernel,
        out_shape=outs,
        in_specs=specs,
        out_specs=[pl.BlockSpec(memory_space=VMEM) for _ in outs],
        compiler_params=pltpu.CompilerParams(vmem_limit_bytes=20 * 2**20),
        cost_estimate=pl.CostEstimate(flops=flops, transcendentals=0, bytes_accessed=moved_bytes),
    )(*args)


def total(kept, sent, update):
    rows, width = kept.shape
    value = kept + moved(sent, 1, 0).astype(F32)
    plane, line = SIZES[0] * SIZES[2] * SIZES[4], SIZES[3]
    piece = value.astype(BF16).reshape(SIZES[0] * SIZES[4], -1, width)
    piece = lax.all_to_all(piece, PLANE[:2], 0, 0, tiled=True)
    piece = jnp.sum(piece.astype(F32), axis=0).astype(BF16)
    piece = piece.reshape(SIZES[2] * line, -1, 128)
    piece = lax.all_to_all(piece, ("x", "z"), 0, 0, tiled=True)
    piece = jnp.sum(piece.astype(F32), axis=0).astype(BF16)
    piece, update = lax.optimization_barrier((piece, update))
    piece = jnp.broadcast_to(piece[None], (line,) + piece.shape)
    piece = lax.all_to_all(piece, "z", 0, 0, tiled=True).reshape(rows // plane, width)
    piece = jnp.broadcast_to(piece[None], (plane,) + piece.shape)
    mine = lax.all_to_all(piece, PLANE, 0, 0, tiled=True).reshape(rows, width)
    return mine, moved(mine, 1, 0), update


def per_device(queries, docids, labels, head_query, head_docid):
    rows, width = queries.shape
    side = head_query.shape[1]
    core = lax.axis_index("core")
    group = lax.axis_index("y_lo") * 2 + core
    dev = (lax.axis_index("x") * 8 + lax.axis_index("z")) * 2 + lax.axis_index("y_hi")
    own_start = (group * DEVS + dev) * rows
    far_start = (group * DEVS + (dev - 2) % DEVS) * rows
    starts = jnp.stack([own_start, far_start, core]).astype(jnp.int32)

    far = moved(docids, 0, 2)
    cut = 384
    row = labels[None]
    queries_2, labels_2 = moved(queries, 2, -2), moved(labels, 2, -2)
    part_a = pack(row, queries, 0, cut)
    queries_1a = moved(part_a, 1, -1)
    rest, part_a = lax.optimization_barrier((queries, part_a))
    queries_1b = moved(pack(row, rest, cut, rows - cut), 1, -1)

    def out(shape, dtype=F32):
        return jax.ShapeDtypeStruct(shape, dtype)

    block, column, head = (rows, side), (rows, 1), (width, side)
    mul = 2 * rows * width * side
    pair_flops = 2 * rows * rows * side
    docid_vec, docid_unit, docid_scale, docid_grad, query_head = call(
        own_kernel,
        [out(block, BF16), out(block), out(column), out(block), out(head)],
        starts, row, queries, docids, head_query, head_docid,
        flops=3 * mul + 3 * pair_flops,
    )
    query_vec, query_unit, query_scale = call(
        query_kernel,
        [out(block, BF16), out(block), out(column)],
        queries_2, head_query,
        flops=4 * mul, scalars=False,
    )
    docid_grad, far_grad, query_head, far_vec, far_unit, far_scale = call(
        first_kernel,
        [out(block), out(block), out(head), out(block, BF16), out(block), out(column)],
        starts, queries_2, labels_2[None], query_vec, query_unit, query_scale, docid_vec, docid_grad, query_head, far, head_docid,
        flops=3 * mul + 6 * pair_flops,
    )
    queries_1a, far_grad = lax.optimization_barrier((queries_1a, far_grad))
    docid_grad, far_grad, query_head = call(
        next_kernel,
        [out(block), out(block), out(head)],
        starts, queries_1a, head_query, docid_vec, docid_grad, query_head, far_vec, far_grad,
        flops=mul + 4 * pair_flops,
    )
    queries_1b, far_grad = lax.optimization_barrier((queries_1b, far_grad))
    docid_grad, far_sent, kept, sent = call(
        last_kernel,
        [out(block), out(block, BF16), out(head), out(head, BF16)],
        starts, queries_1b, head_query, docid_vec, docid_grad, query_head, far_vec, far_grad,
        docids, docid_unit, docid_scale, far, far_unit, far_scale,
        flops=3 * mul + 4 * pair_flops,
    )
    back = moved(far_sent, 0, -2)
    (doc_update,) = call(
        update_kernel,
        [out((rows, width), BF16)],
        docid_grad, back, docid_unit, docid_scale, head_docid,
        flops=40 * mul, scalars=False,
    )
    mine, other, doc_update = total(kept, sent, doc_update)
    query_step, docid_step = steps(starts, mine, other)
    return (doc_update, query_step, docid_step)


def solution(mesh):
    split = Mesh(mesh.devices.reshape(SIZES), AXES)
    rows = P(AXES)
    return jax.shard_map(
        per_device,
        mesh=split,
        in_specs=(rows, rows, rows, P(), P()),
        out_specs=(rows, P(), P()),
        check_vma=False,
    )
```

```python
import functools

import jax
import jax.numpy as jnp
from jax import lax
from jax.experimental import pallas as pl
from jax.experimental.pallas import tpu as pltpu
from jax.sharding import Mesh
from jax.sharding import PartitionSpec as P

LOGIT_SCALE = 5.0
LOGIT_BIAS = -2.0
EPSILON = 1e-06

AXES = ("y_lo", "core", "x", "z", "y_hi")
SIZES = (2, 2, 4, 8, 2)
PLANE = ("y_lo", "y_hi", "x")
DEVS = 64
F32, BF16 = jnp.float32, jnp.bfloat16
VMEM, SMEM = pltpu.VMEM, pltpu.SMEM


def moved(block, flip, shift):
    pairs = []
    for source in range(4 * DEVS):
        group, dev = divmod(source, DEVS)
        pairs.append((source, (group ^ flip) * DEVS + (dev + shift) % DEVS))
    return lax.ppermute(block, AXES, pairs)


def dot(a, b, contract):
    return lax.dot_general(a, b, (contract, ((), ())), preferred_element_type=F32)


PLAIN, ROWS, COLUMNS = ((1,), (0,)), ((1,), (1,)), ((0,), (0,))


def project(inputs, weight):
    projected = dot(inputs, weight, PLAIN)
    inverse = lax.rsqrt(jnp.sum(projected * projected, axis=-1, keepdims=True) + EPSILON)
    return (projected * inverse, inverse)


def direction(grad, unit, scale):
    inner = jnp.sum(unit * grad, axis=-1, keepdims=True)
    return ((grad - unit * inner) * scale).astype(BF16)


def pair_weights(docids, queries, labels, doc_start):
    logits = LOGIT_SCALE * dot(docids, queries, ROWS) + LOGIT_BIAS
    rows = doc_start + lax.broadcasted_iota(jnp.int32, logits.shape, 0)
    return (jax.nn.sigmoid(logits) - jnp.where(labels == rows, 1.0, 0.0)).astype(BF16)


def pack_kernel(start, labels, queries, packed):
    count = packed.shape[0] - 16
    packed[0:count, :] = queries[start : start + count, :]
    label = labels[:, start : start + count]
    row = lax.broadcasted_iota(jnp.int32, (16, count), 0)
    digit = jnp.where(row == 0, label & 63, jnp.where(row == 1, (label >> 6) & 63, label >> 12))
    packed[count : count + 16, :] = jnp.zeros((16, packed.shape[1]), BF16)
    packed[count : count + 16, 0:count] = jnp.where(row < 3, digit, 0).astype(F32).astype(BF16)


def pack(labels, queries, start, count):
    (packed,) = call(
        functools.partial(pack_kernel, start),
        [jax.ShapeDtypeStruct((count + 16, queries.shape[1]), BF16)],
        labels, queries,
        scalars=False,
    )
    return packed


def unpacked(part):
    count = part.shape[0] - 16
    digits = part[count : count + 16, 0:count].astype(F32)
    labels = digits[0:1] + 64.0 * digits[1:2] + 4096.0 * digits[2:3]
    return part[0:count, :], labels.astype(jnp.int32)


def own_kernel(starts, labels, queries, docids, head_query, head_docid,
               docid_vec, docid_unit, docid_scale, docid_grad, query_head):
    unit, inverse = project(docids[...], head_docid[...])
    docid_unit[...] = unit
    docid_scale[...] = LOGIT_SCALE * inverse
    vec = unit.astype(BF16)
    docid_vec[...] = vec
    unit, inverse = project(queries[...], head_query[...])
    query_vec = unit.astype(BF16)
    weights = pair_weights(vec, query_vec, labels[...], starts[0])
    docid_grad[...] = dot(weights, query_vec, PLAIN)
    query_grad = dot(weights, vec, COLUMNS)
    query_head[...] = dot(queries[...], direction(query_grad, unit, LOGIT_SCALE * inverse), COLUMNS)


def query_kernel(queries, head_query, query_vec, query_unit, query_scale):
    unit, inverse = project(queries[...], head_query[...])
    query_unit[...] = unit
    query_scale[...] = LOGIT_SCALE * inverse
    query_vec[...] = unit.astype(BF16)


def scored(starts, queries, labels, query_vec, unit, scale, docid_vec, far_vec):
    weights = pair_weights(far_vec, query_vec, labels, starts[1])
    far_grad = dot(weights, query_vec, PLAIN)
    query_grad = dot(weights, far_vec, COLUMNS)
    weights = pair_weights(docid_vec, query_vec, labels, starts[0])
    docid_grad = dot(weights, query_vec, PLAIN)
    query_grad = query_grad + dot(weights, docid_vec, COLUMNS)
    head = dot(queries, direction(query_grad, unit, scale), COLUMNS)
    return docid_grad, far_grad, head


def pair(starts, queries, labels, head_query, docid_vec, far_vec):
    unit, inverse = project(queries, head_query[...])
    return scored(starts, queries, labels, unit.astype(BF16), unit, LOGIT_SCALE * inverse, docid_vec, far_vec)


def first_kernel(starts, queries, labels, query_vec, query_unit, query_scale, docid_vec, docid_in, head_in, far, head_docid,
                 docid_out, far_out, head_out, far_vec, far_unit, far_scale):
    unit, inverse = project(far[...], head_docid[...])
    far_unit[...] = unit
    far_scale[...] = LOGIT_SCALE * inverse
    vec = unit.astype(BF16)
    far_vec[...] = vec
    docid_grad, far_out[...], head = scored(
        starts, queries[...], labels[...], query_vec[...], query_unit[...], query_scale[...], docid_vec[...], vec
    )
    docid_out[...] = docid_in[...] + docid_grad
    head_out[...] = head_in[...] + head


def next_kernel(starts, part, head_query, docid_vec, docid_in, head_in, far_vec, far_in,
                docid_out, far_out, head_out):
    docid_grad, far_grad, head = pair(starts, *unpacked(part), head_query, docid_vec[...], far_vec[...])
    docid_out[...] = docid_in[...] + docid_grad
    far_out[...] = far_in[...] + far_grad
    head_out[...] = head_in[...] + head


def last_kernel(starts, part, head_query, docid_vec, docid_in, head_in, far_vec, far_in,
                docids, docid_unit, docid_scale, far, far_unit, far_scale,
                docid_out, far_sent, kept, sent):
    docid_grad, far_grad, query = pair(starts, *unpacked(part), head_query, docid_vec[...], far_vec[...])
    docid_grad = docid_grad + docid_in[...]
    far_grad = far_grad + far_in[...]
    query = query + head_in[...]
    docid_out[...] = docid_grad
    far_sent[...] = far_grad.astype(BF16)
    own_direct = direction(docid_grad, docid_unit[...], docid_scale[...])
    far_direct = direction(far_grad, far_unit[...], far_scale[...])
    rows = jnp.concatenate([docids[...], far[...]])
    head = dot(rows, jnp.concatenate([own_direct, far_direct]), COLUMNS)
    mine = jnp.zeros(head.shape, jnp.int32) + starts[2] == 0
    kept[...] = jnp.where(mine, query, head)
    sent[...] = jnp.where(mine, head, query).astype(BF16)


def update_kernel(docid_grad, back, docid_unit, docid_scale, head_docid, update):
    grad = docid_grad[...] + back[...].astype(F32)
    direct = direction(grad, docid_unit[...], docid_scale[...])
    grad = dot(direct, head_docid[...], ROWS)
    scale = lax.rsqrt(jnp.mean(grad * grad, axis=-1, keepdims=True) + EPSILON)
    update[...] = (grad * scale).astype(BF16)


def rms_scale(grad):
    grad = grad.astype(F32)
    return lax.rsqrt(jnp.sum(grad * grad) / (grad.shape[0] * grad.shape[1]) + EPSILON)


def write(head, target, staged, sems):
    depth, block = staged.shape[0], staged.shape[1]
    scale = rms_scale(head[...])
    copies = []
    for step in range(depth):
        rows = slice(step * block, (step + 1) * block)
        staged[step] = head[rows, :].astype(F32) * scale
        copies.append(pltpu.make_async_copy(staged.at[step], target.at[rows], sems.at[step]))
        copies[-1].start()
    for copy in copies:
        copy.wait()


def mine_kernel(starts, mine, query_step, docid_step, staged, sems):
    @pl.when(starts[2] == 0)
    def _():
        write(mine, query_step, staged, sems)

    @pl.when(starts[2] != 0)
    def _():
        write(mine, docid_step, staged, sems)


def other_kernel(starts, other, query_in, docid_in, query_step, docid_step, staged, sems):
    del query_in, docid_in

    @pl.when(starts[2] == 0)
    def _():
        write(other, docid_step, staged, sems)

    @pl.when(starts[2] != 0)
    def _():
        write(other, query_step, staged, sems)


def steps(starts, mine, other):
    rows, width = mine.shape
    depth = 3
    outside = pl.BlockSpec(memory_space=pltpu.HBM)
    common = dict(
        out_shape=[jax.ShapeDtypeStruct((rows, width), F32)] * 2,
        out_specs=[outside] * 2,
        scratch_shapes=[VMEM((depth, rows // depth, width), F32), pltpu.SemaphoreType.DMA((depth,))],
        compiler_params=pltpu.CompilerParams(vmem_limit_bytes=24 * 2**20),
    )
    given = [pl.BlockSpec(memory_space=SMEM), pl.BlockSpec(memory_space=VMEM)]
    written = pl.pallas_call(mine_kernel, in_specs=given, **common)(starts, mine)
    return pl.pallas_call(
        other_kernel, in_specs=given + [outside] * 2, input_output_aliases={2: 0, 3: 1}, **common
    )(starts, other, *written)


def call(kernel, outs, *args, flops=0, scalars=True):
    specs = [pl.BlockSpec(memory_space=VMEM) for _ in args]
    if scalars:
        specs[0] = pl.BlockSpec(memory_space=SMEM)
    moved_bytes = sum(a.size * a.dtype.itemsize for a in args)
    moved_bytes += sum(o.size * o.dtype.itemsize for o in outs)
    return pl.pallas_call(
        kernel,
        out_shape=outs,
        in_specs=specs,
        out_specs=[pl.BlockSpec(memory_space=VMEM) for _ in outs],
        compiler_params=pltpu.CompilerParams(vmem_limit_bytes=20 * 2**20),
        cost_estimate=pl.CostEstimate(flops=flops, transcendentals=0, bytes_accessed=moved_bytes),
    )(*args)


def total(kept, sent, update):
    rows, width = kept.shape
    value = kept + moved(sent, 1, 0).astype(F32)
    plane, line = SIZES[0] * SIZES[2] * SIZES[4], SIZES[3]
    piece = value.astype(BF16).reshape(SIZES[0] * SIZES[4], -1, width)
    piece = lax.all_to_all(piece, PLANE[:2], 0, 0, tiled=True)
    piece = jnp.sum(piece.astype(F32), axis=0).astype(BF16)
    piece = piece.reshape(SIZES[2] * line, -1, 128)
    piece = lax.all_to_all(piece, ("x", "z"), 0, 0, tiled=True)
    piece = jnp.sum(piece.astype(F32), axis=0).astype(BF16)
    piece, update = lax.optimization_barrier((piece, update))
    piece = jnp.broadcast_to(piece[None], (line,) + piece.shape)
    piece = lax.all_to_all(piece, "z", 0, 0, tiled=True).reshape(rows // plane, width)
    piece = jnp.broadcast_to(piece[None], (plane,) + piece.shape)
    mine = lax.all_to_all(piece, PLANE, 0, 0, tiled=True).reshape(rows, width)
    return mine, moved(mine, 1, 0), update


def per_device(queries, docids, labels, head_query, head_docid):
    rows, width = queries.shape
    side = head_query.shape[1]
    core = lax.axis_index("core")
    group = lax.axis_index("y_lo") * 2 + core
    dev = (lax.axis_index("x") * 8 + lax.axis_index("z")) * 2 + lax.axis_index("y_hi")
    own_start = (group * DEVS + dev) * rows
    far_start = (group * DEVS + (dev - 2) % DEVS) * rows
    starts = jnp.stack([own_start, far_start, core]).astype(jnp.int32)

    far = moved(docids, 0, 2)
    cut = 384
    row = labels[None]
    queries_2, labels_2 = moved(queries, 2, -2), moved(labels, 2, -2)
    part_a = pack(row, queries, 0, cut)
    queries_1a = moved(part_a, 1, -1)
    rest, part_a = lax.optimization_barrier((queries, part_a))
    queries_1b = moved(pack(row, rest, cut, rows - cut), 1, -1)

    def out(shape, dtype=F32):
        return jax.ShapeDtypeStruct(shape, dtype)

    block, column, head = (rows, side), (rows, 1), (width, side)
    mul = 2 * rows * width * side
    pair_flops = 2 * rows * rows * side
    docid_vec, docid_unit, docid_scale, docid_grad, query_head = call(
        own_kernel,
        [out(block, BF16), out(block), out(column), out(block), out(head)],
        starts, row, queries, docids, head_query, head_docid,
        flops=3 * mul + 3 * pair_flops,
    )
    query_vec, query_unit, query_scale = call(
        query_kernel,
        [out(block, BF16), out(block), out(column)],
        queries_2, head_query,
        flops=4 * mul, scalars=False,
    )
    docid_grad, far_grad, query_head, far_vec, far_unit, far_scale = call(
        first_kernel,
        [out(block), out(block), out(head), out(block, BF16), out(block), out(column)],
        starts, queries_2, labels_2[None], query_vec, query_unit, query_scale, docid_vec, docid_grad, query_head, far, head_docid,
        flops=3 * mul + 6 * pair_flops,
    )
    queries_1a, far_grad = lax.optimization_barrier((queries_1a, far_grad))
    docid_grad, far_grad, query_head = call(
        next_kernel,
        [out(block), out(block), out(head)],
        starts, queries_1a, head_query, docid_vec, docid_grad, query_head, far_vec, far_grad,
        flops=mul + 4 * pair_flops,
    )
    queries_1b, far_grad = lax.optimization_barrier((queries_1b, far_grad))
    docid_grad, far_sent, kept, sent = call(
        last_kernel,
        [out(block), out(block, BF16), out(head), out(head, BF16)],
        starts, queries_1b, head_query, docid_vec, docid_grad, query_head, far_vec, far_grad,
        docids, docid_unit, docid_scale, far, far_unit, far_scale,
        flops=3 * mul + 4 * pair_flops,
    )
    back = moved(far_sent, 0, -2)
    (doc_update,) = call(
        update_kernel,
        [out((rows, width), BF16)],
        docid_grad, back, docid_unit, docid_scale, head_docid,
        flops=40 * mul, scalars=False,
    )
    mine, other, doc_update = total(kept, sent, doc_update)
    query_step, docid_step = steps(starts, mine, other)
    return (doc_update, query_step, docid_step)


def solution(mesh):
    split = Mesh(mesh.devices.reshape(SIZES), AXES)
    rows = P(AXES)
    return jax.shard_map(
        per_device,
        mesh=split,
        in_specs=(rows, rows, rows, P(), P()),
        out_specs=(rows, P(), P()),
        check_vma=False,
    )
```

```python
import functools

import jax
import jax.numpy as jnp
from jax import lax
from jax.experimental import pallas as pl
from jax.experimental.pallas import tpu as pltpu
from jax.sharding import Mesh
from jax.sharding import PartitionSpec as P

LOGIT_SCALE = 5.0
LOGIT_BIAS = -2.0
EPSILON = 1e-06

AXES = ("y_lo", "core", "x", "z", "y_hi")
SIZES = (2, 2, 4, 8, 2)
PLANE = ("y_lo", "y_hi", "x")
DEVS = 64
F32, BF16 = jnp.float32, jnp.bfloat16
VMEM, SMEM = pltpu.VMEM, pltpu.SMEM


def moved(block, flip, shift):
    pairs = []
    for source in range(4 * DEVS):
        group, dev = divmod(source, DEVS)
        pairs.append((source, (group ^ flip) * DEVS + (dev + shift) % DEVS))
    return lax.ppermute(block, AXES, pairs)


def dot(a, b, contract):
    return lax.dot_general(a, b, (contract, ((), ())), preferred_element_type=F32)


PLAIN, ROWS, COLUMNS = ((1,), (0,)), ((1,), (1,)), ((0,), (0,))


def project(inputs, weight):
    projected = dot(inputs, weight, PLAIN)
    inverse = lax.rsqrt(jnp.sum(projected * projected, axis=-1, keepdims=True) + EPSILON)
    return (projected * inverse, inverse)


def direction(grad, unit, scale):
    inner = jnp.sum(unit * grad, axis=-1, keepdims=True)
    return ((grad - unit * inner) * scale).astype(BF16)


def pair_weights(docids, queries, labels, doc_start):
    logits = LOGIT_SCALE * dot(docids, queries, ROWS) + LOGIT_BIAS
    rows = doc_start + lax.broadcasted_iota(jnp.int32, logits.shape, 0)
    return (jax.nn.sigmoid(logits) - jnp.where(labels == rows, 1.0, 0.0)).astype(BF16)


def pack_kernel(start, labels, queries, packed):
    count = packed.shape[0] - 16
    packed[0:count, :] = queries[start : start + count, :]
    label = labels[:, start : start + count]
    row = lax.broadcasted_iota(jnp.int32, (16, count), 0)
    digit = jnp.where(row == 0, label & 63, jnp.where(row == 1, (label >> 6) & 63, label >> 12))
    packed[count : count + 16, :] = jnp.zeros((16, packed.shape[1]), BF16)
    packed[count : count + 16, 0:count] = jnp.where(row < 3, digit, 0).astype(F32).astype(BF16)


def pack(labels, queries, start, count):
    (packed,) = call(
        functools.partial(pack_kernel, start),
        [jax.ShapeDtypeStruct((count + 16, queries.shape[1]), BF16)],
        labels, queries,
        scalars=False,
    )
    return packed


def unpacked(part):
    count = part.shape[0] - 16
    digits = part[count : count + 16, 0:count].astype(F32)
    labels = digits[0:1] + 64.0 * digits[1:2] + 4096.0 * digits[2:3]
    return part[0:count, :], labels.astype(jnp.int32)


def own_kernel(starts, labels, queries, docids, head_query, head_docid,
               docid_vec, docid_unit, docid_scale, docid_grad, query_head):
    unit, inverse = project(docids[...], head_docid[...])
    docid_unit[...] = unit
    docid_scale[...] = LOGIT_SCALE * inverse
    vec = unit.astype(BF16)
    docid_vec[...] = vec
    unit, inverse = project(queries[...], head_query[...])
    query_vec = unit.astype(BF16)
    weights = pair_weights(vec, query_vec, labels[...], starts[0])
    docid_grad[...] = dot(weights, query_vec, PLAIN)
    query_grad = dot(weights, vec, COLUMNS)
    query_head[...] = dot(queries[...], direction(query_grad, unit, LOGIT_SCALE * inverse), COLUMNS)


def pair(starts, queries, labels, head_query, docid_vec, far_vec):
    unit, inverse = project(queries, head_query[...])
    query_vec = unit.astype(BF16)
    weights = pair_weights(far_vec, query_vec, labels, starts[1])
    far_grad = dot(weights, query_vec, PLAIN)
    query_grad = dot(weights, far_vec, COLUMNS)
    weights = pair_weights(docid_vec, query_vec, labels, starts[0])
    docid_grad = dot(weights, query_vec, PLAIN)
    query_grad = query_grad + dot(weights, docid_vec, COLUMNS)
    head = dot(queries, direction(query_grad, unit, LOGIT_SCALE * inverse), COLUMNS)
    return docid_grad, far_grad, head


def first_kernel(starts, queries, labels, head_query, docid_vec, docid_in, head_in, far, head_docid,
                 docid_out, far_out, head_out, far_vec, far_unit, far_scale):
    unit, inverse = project(far[...], head_docid[...])
    far_unit[...] = unit
    far_scale[...] = LOGIT_SCALE * inverse
    vec = unit.astype(BF16)
    far_vec[...] = vec
    docid_grad, far_out[...], head = pair(starts, queries[...], labels[...], head_query, docid_vec[...], vec)
    docid_out[...] = docid_in[...] + docid_grad
    head_out[...] = head_in[...] + head


def next_kernel(starts, part, head_query, docid_vec, docid_in, head_in, far_vec, far_in,
                docid_out, far_out, head_out):
    docid_grad, far_grad, head = pair(starts, *unpacked(part), head_query, docid_vec[...], far_vec[...])
    docid_out[...] = docid_in[...] + docid_grad
    far_out[...] = far_in[...] + far_grad
    head_out[...] = head_in[...] + head


def last_kernel(starts, part, head_query, docid_vec, docid_in, head_in, far_vec, far_in,
                docids, docid_unit, docid_scale, far, far_unit, far_scale,
                docid_out, far_sent, kept, sent):
    docid_grad, far_grad, query = pair(starts, *unpacked(part), head_query, docid_vec[...], far_vec[...])
    docid_grad = docid_grad + docid_in[...]
    far_grad = far_grad + far_in[...]
    query = query + head_in[...]
    docid_out[...] = docid_grad
    far_sent[...] = far_grad.astype(BF16)
    head = dot(docids[...], direction(docid_grad, docid_unit[...], docid_scale[...]), COLUMNS)
    head = head + dot(far[...], direction(far_grad, far_unit[...], far_scale[...]), COLUMNS)
    mine = jnp.zeros(head.shape, jnp.int32) + starts[2] == 0
    kept[...] = jnp.where(mine, query, head)
    sent[...] = jnp.where(mine, head, query).astype(BF16)


def update_kernel(docid_grad, back, docid_unit, docid_scale, head_docid, update):
    grad = docid_grad[...] + back[...].astype(F32)
    direct = direction(grad, docid_unit[...], docid_scale[...])
    grad = dot(direct, head_docid[...], ROWS)
    scale = lax.rsqrt(jnp.mean(grad * grad, axis=-1, keepdims=True) + EPSILON)
    update[...] = (grad * scale).astype(BF16)


def rms_scale(grad):
    grad = grad.astype(F32)
    return lax.rsqrt(jnp.sum(grad * grad) / (grad.shape[0] * grad.shape[1]) + EPSILON)


def write(head, target, staged, sems):
    depth, block = staged.shape[0], staged.shape[1]
    scale = rms_scale(head[...])
    copies = []
    for step in range(depth):
        rows = slice(step * block, (step + 1) * block)
        staged[step] = head[rows, :].astype(F32) * scale
        copies.append(pltpu.make_async_copy(staged.at[step], target.at[rows], sems.at[step]))
        copies[-1].start()
    for copy in copies:
        copy.wait()


def mine_kernel(starts, mine, query_step, docid_step, staged, sems):
    @pl.when(starts[2] == 0)
    def _():
        write(mine, query_step, staged, sems)

    @pl.when(starts[2] != 0)
    def _():
        write(mine, docid_step, staged, sems)


def other_kernel(starts, other, query_in, docid_in, query_step, docid_step, staged, sems):
    del query_in, docid_in

    @pl.when(starts[2] == 0)
    def _():
        write(other, docid_step, staged, sems)

    @pl.when(starts[2] != 0)
    def _():
        write(other, query_step, staged, sems)


def steps(starts, mine, other):
    rows, width = mine.shape
    depth = 3
    outside = pl.BlockSpec(memory_space=pltpu.HBM)
    common = dict(
        out_shape=[jax.ShapeDtypeStruct((rows, width), F32)] * 2,
        out_specs=[outside] * 2,
        scratch_shapes=[VMEM((depth, rows // depth, width), F32), pltpu.SemaphoreType.DMA((depth,))],
        compiler_params=pltpu.CompilerParams(vmem_limit_bytes=24 * 2**20),
    )
    given = [pl.BlockSpec(memory_space=SMEM), pl.BlockSpec(memory_space=VMEM)]
    written = pl.pallas_call(mine_kernel, in_specs=given, **common)(starts, mine)
    return pl.pallas_call(
        other_kernel, in_specs=given + [outside] * 2, input_output_aliases={2: 0, 3: 1}, **common
    )(starts, other, *written)


def call(kernel, outs, *args, flops=0, scalars=True):
    specs = [pl.BlockSpec(memory_space=VMEM) for _ in args]
    if scalars:
        specs[0] = pl.BlockSpec(memory_space=SMEM)
    moved_bytes = sum(a.size * a.dtype.itemsize for a in args)
    moved_bytes += sum(o.size * o.dtype.itemsize for o in outs)
    return pl.pallas_call(
        kernel,
        out_shape=outs,
        in_specs=specs,
        out_specs=[pl.BlockSpec(memory_space=VMEM) for _ in outs],
        compiler_params=pltpu.CompilerParams(vmem_limit_bytes=20 * 2**20),
        cost_estimate=pl.CostEstimate(flops=flops, transcendentals=0, bytes_accessed=moved_bytes),
    )(*args)


def total(kept, sent, update):
    rows, width = kept.shape
    value = kept + moved(sent, 1, 0).astype(F32)
    plane, line = SIZES[0] * SIZES[2] * SIZES[4], SIZES[3]
    piece = value.astype(BF16).reshape(SIZES[0] * SIZES[4], -1, width)
    piece = lax.all_to_all(piece, PLANE[:2], 0, 0, tiled=True)
    piece = jnp.sum(piece.astype(F32), axis=0).astype(BF16)
    piece = piece.reshape(SIZES[2] * line, -1, width)
    piece = lax.all_to_all(piece, ("x", "z"), 0, 0, tiled=True)
    piece = jnp.sum(piece.astype(F32), axis=0).astype(BF16)
    piece, update = lax.optimization_barrier((piece, update))
    piece = jnp.broadcast_to(piece[None], (line,) + piece.shape)
    piece = lax.all_to_all(piece, "z", 0, 0, tiled=True).reshape(rows // plane, width)
    piece = jnp.broadcast_to(piece[None], (plane,) + piece.shape)
    mine = lax.all_to_all(piece, PLANE, 0, 0, tiled=True).reshape(rows, width)
    return mine, moved(mine, 1, 0), update


def per_device(queries, docids, labels, head_query, head_docid):
    rows, width = queries.shape
    side = head_query.shape[1]
    core = lax.axis_index("core")
    group = lax.axis_index("y_lo") * 2 + core
    dev = (lax.axis_index("x") * 8 + lax.axis_index("z")) * 2 + lax.axis_index("y_hi")
    own_start = (group * DEVS + dev) * rows
    far_start = (group * DEVS + (dev - 2) % DEVS) * rows
    starts = jnp.stack([own_start, far_start, core]).astype(jnp.int32)

    far = moved(docids, 0, 2)
    cut = 384
    row = labels[None]
    queries_2, labels_2 = moved(queries, 2, -2), moved(labels, 2, -2)
    part_a = pack(row, queries, 0, cut)
    queries_1a = moved(part_a, 1, -1)
    rest, part_a = lax.optimization_barrier((queries, part_a))
    queries_1b = moved(pack(row, rest, cut, rows - cut), 1, -1)

    def out(shape, dtype=F32):
        return jax.ShapeDtypeStruct(shape, dtype)

    block, column, head = (rows, side), (rows, 1), (width, side)
    mul = 2 * rows * width * side
    pair_flops = 2 * rows * rows * side
    docid_vec, docid_unit, docid_scale, docid_grad, query_head = call(
        own_kernel,
        [out(block, BF16), out(block), out(column), out(block), out(head)],
        starts, row, queries, docids, head_query, head_docid,
        flops=3 * mul + 3 * pair_flops,
    )
    docid_grad, far_grad, query_head, far_vec, far_unit, far_scale = call(
        first_kernel,
        [out(block), out(block), out(head), out(block, BF16), out(block), out(column)],
        starts, queries_2, labels_2[None], head_query, docid_vec, docid_grad, query_head, far, head_docid,
        flops=3 * mul + 6 * pair_flops,
    )
    queries_1a, far_grad = lax.optimization_barrier((queries_1a, far_grad))
    docid_grad, far_grad, query_head = call(
        next_kernel,
        [out(block), out(block), out(head)],
        starts, queries_1a, head_query, docid_vec, docid_grad, query_head, far_vec, far_grad,
        flops=mul + 4 * pair_flops,
    )
    queries_1b, far_grad = lax.optimization_barrier((queries_1b, far_grad))
    docid_grad, far_sent, kept, sent = call(
        last_kernel,
        [out(block), out(block, BF16), out(head), out(head, BF16)],
        starts, queries_1b, head_query, docid_vec, docid_grad, query_head, far_vec, far_grad,
        docids, docid_unit, docid_scale, far, far_unit, far_scale,
        flops=3 * mul + 4 * pair_flops,
    )
    back = moved(far_sent, 0, -2)
    (doc_update,) = call(
        update_kernel,
        [out((rows, width), BF16)],
        docid_grad, back, docid_unit, docid_scale, head_docid,
        flops=40 * mul, scalars=False,
    )
    mine, other, doc_update = total(kept, sent, doc_update)
    query_step, docid_step = steps(starts, mine, other)
    return (doc_update, query_step, docid_step)


def solution(mesh):
    split = Mesh(mesh.devices.reshape(SIZES), AXES)
    rows = P(AXES)
    return jax.shard_map(
        per_device,
        mesh=split,
        in_specs=(rows, rows, rows, P(), P()),
        out_specs=(rows, P(), P()),
        check_vma=False,
    )
```
